32 devices in a mesh: grp: 4 (over y, core), shard: 8 (over z, x).
Axes of the slice: x: 2, y: 2, z: 4, core: 2. Of those that a mesh axis runs over, the one named last changes fastest.
Arguments:
- layer_inner: float32 [4, 1600, 1600], P('grp', 'shard'), may hold values from -6 to 6
- layer_weights: float32 [1600, 1600], P('shard'), may hold values from -6 to 6
- layer_moment: float32 [1600, 1600], P('shard'), may hold values from -6 to 6
- embed_inner: float32 [4, 3200, 1600], P('grp', 'shard'), may hold values from -6 to 6
- embed_weights: float32 [3200, 1600], P(('shard', 'grp')), may hold values from -6 to 6
- embed_moment: float32 [3200, 1600], P(('shard', 'grp')), may hold values from -6 to 6
- basis: float32 [1600, 64], replicated, may hold values from -0.15625 to 0.15625
Outputs:
- layer_new: float32 [1600, 1600], P('shard')
- layer_moment_new: float32 [1600, 1600], P('shard')
- layer_copy: bfloat16 [1600, 1600], replicated
- embed_new: float32 [3200, 1600], P(('shard', 'grp'))
- embed_moment_new: float32 [3200, 1600], P(('shard', 'grp'))
The draws below stay inside these ranges and needn't reach their ends.
All inputs are finite; a program needn't handle non-finite values.
Results may differ from the reference program's by a relative error of at most 0.0015.
Values may be sent and summed in bfloat16 or wider, within the bound.
A program may use at most 128 MiB of HBM per device.

```python
import jax
import jax.numpy as jnp
from jax import lax

D = 1600
RANK = 64
VOCAB = 3200
GROUPS = 4


def block_levels(stream_key, extent, split, smallest, largest):
    level, own = 1.0, jax.random.fold_in(stream_key, 6)
    for dim, shards_of in split:
        steps = jnp.exp(jax.random.uniform(jax.random.fold_in(own, dim), (shards_of,), jnp.float32, smallest / len(split), largest / len(split)))
        level = level * jnp.repeat(steps, extent[dim] // shards_of).reshape([-1 if axis == dim else 1 for axis in range(len(extent))])
    return level


def noise(stream_key, extent, width, most, cuts=(), kind=jnp.bfloat16):
    array = jax.random.normal(stream_key, extent, jnp.float32) * width
    if len(cuts) > 0:
        array = block_levels(stream_key, extent, cuts, -0.22, 0.18) * array
    return jnp.clip(array, min=-most, max=most).astype(kind)


def setup_inputs(seed: int = 0) -> dict:
    streams_of = jax.random.split(jax.random.key(seed), 8)
    return {
        "layer_inner": noise(streams_of[0], (GROUPS, D, D), 1.0, 6.0, ((0, 4), (1, 8)), jnp.float32),
        "layer_weights": noise(streams_of[1], (D, D), 1.0, 6.0, ((0, 8),), jnp.float32),
        "layer_moment": noise(streams_of[2], (D, D), 1.0, 6.0, ((0, 8),), jnp.float32),
        "embed_inner": noise(streams_of[3], (GROUPS, VOCAB, D), 1.0, 6.0, ((0, 4), (1, 8)), jnp.float32),
        "embed_weights": noise(streams_of[4], (VOCAB, D), 1.0, 6.0, ((0, 32),), jnp.float32),
        "embed_moment": noise(streams_of[5], (VOCAB, D), 1.0, 6.0, ((0, 32),), jnp.float32),
        "basis": noise(streams_of[6], (D, RANK), D ** -0.5, 0.15625, (), jnp.float32),
    }


outer_rate = 0.7
momentum_coef = 0.9


def nesterov(weights, moment, average):
    moment_new = momentum_coef * moment + average
    return weights - outer_rate * (average + momentum_coef * moment_new), moment_new


def reference(layer_inner, layer_weights, layer_moment, embed_inner, embed_weights, embed_moment, basis):
    layer_delta = jnp.mean(layer_weights[None] - layer_inner, axis=0)
    layer_new, layer_moment_new = nesterov(layer_weights, layer_moment, layer_delta)
    layer_copy = layer_new.astype(jnp.bfloat16)
    differences = embed_weights[None] - embed_inner
    projected = jnp.einsum("gvd,dr->gvr", differences, basis, precision=lax.Precision.HIGHEST)
    factors = jnp.mean(projected, axis=0)
    embed_delta = jnp.dot(factors, basis.T, precision=lax.Precision.HIGHEST)
    embed_new, embed_moment_new = nesterov(embed_weights, embed_moment, embed_delta)
    return layer_new, layer_moment_new, layer_copy, embed_new, embed_moment_new
```

```python
import functools

import jax
import jax.numpy as jnp
from jax import lax
from jax.experimental import pallas as pl
from jax.experimental.pallas import tpu as pltpu
from jax.sharding import PartitionSpec as P

outer_rate = 0.7
momentum_coef = 0.9
MESH = pl.DeviceIdType.MESH
LANES = 128
SLOPE = 13.0
SHIFT = 78.0


def nesterov(weights, moment, average):
    moment_new = momentum_coef * moment + average
    return (weights - outer_rate * (average + momentum_coef * moment_new), moment_new)


def encode(x):
    size = jnp.exp(jnp.abs(x) * SLOPE - SHIFT)
    return jnp.where(x < 0, -size, size).astype(jnp.bfloat16)


def decode(code):
    code = code.astype(jnp.float32)
    size = (jnp.log(jnp.abs(code)) + SHIFT) * (1.0 / SLOPE)
    return jnp.where(code < 0, -size, size)


def kernel(
    zs, groups, quarter,
    inner_h, w_h, m_h, einner_h, ew_h, em_h, bt_h,
    new_h, mom_h, all_h, enew_h, emom_h,
    inner, sib, w, m, einner, ew, em, bt, code, rcode, own, new, mom, proj, precv, enew, emom,
    in_sem, out_sem, a1_s, a1_r, a2_s, a2_r, a2f_s, a2f_r, e_s, e_r,
    up_s, dn_s, z_r, x_s, x_r, y_s, y_r, cz_s, cz_r, cx_s, cx_r, cy_s, cy_r,
):
    g, s = lax.axis_index("grp"), lax.axis_index("shard")
    y, c = g // 2, g % 2
    z, x = s // 2, s % 2
    width = inner_h.shape[-1]
    rows_e = ew_h.shape[0]
    tail0 = 4 * quarter
    tail_w = own.shape[-1] - tail0
    sib_id = (y * 2 + 1 - c, s)
    y_id = ((1 - y) * 2 + c, s)
    diag_id = ((1 - y) * 2 + 1 - c, s)
    x_id = (g, z * 2 + 1 - x)
    up_id = (g, s + 2)
    dn_id = (g, s - 2)
    has_up, has_dn = z < zs - 1, z > 0

    loads = [
        pltpu.make_async_copy(src, dst, in_sem.at[i])
        for i, (src, dst) in enumerate(
            [(inner_h.at[0], inner), (einner_h.at[0], einner), (bt_h, bt), (w_h, w), (m_h, m), (ew_h, ew), (em_h, em)]
        )
    ]
    for load in loads:
        load.start()

    barrier = pltpu.get_barrier_semaphore()
    for peer in (sib_id, y_id, diag_id, x_id):
        pl.semaphore_signal(barrier, inc=1, device_id=peer, device_id_type=MESH)

    @pl.when(has_up)
    def _():
        pl.semaphore_signal(barrier, inc=1, device_id=up_id, device_id_type=MESH)

    @pl.when(has_dn)
    def _():
        pl.semaphore_signal(barrier, inc=1, device_id=dn_id, device_id_type=MESH)

    pl.semaphore_wait(barrier, 4 + has_up.astype(jnp.int32) + has_dn.astype(jnp.int32))

    def remote(src, dst, ssem, rsem, peer):
        return pltpu.make_async_remote_copy(
            src_ref=src, dst_ref=dst, send_sem=ssem, recv_sem=rsem, device_id=peer, device_id_type=MESH
        )

    a1 = remote(inner_h.at[0], sib, a1_s, a1_r, sib_id)
    a1.start()
    loads[0].wait()
    a1.wait_recv()
    code[:, :tail0] = encode(inner[:, :tail0] + sib[:, :tail0])
    code[:, tail0:] = jnp.zeros_like(code[:, tail0:])
    code[:, tail0:width] = encode(inner[:, tail0:] + sib[:, tail0:])

    def cols(core, k):
        if k == 2:
            return pl.ds(tail0, tail_w)
        return pl.ds(pl.multiple_of((core * 2 + (y if k == 0 else 1 - y)) * quarter, LANES), quarter)

    def when_tail(core, k, f):
        if k == 2:
            pl.when(core == 1)(f)
        else:
            f()

    def a2(k):
        at = cols(c, 1 - k if k < 2 else 2)
        return remote(code.at[:, at], rcode.at[:, at], a2_s.at[k], a2_r.at[k], y_id)

    def a2_in(k):
        at = cols(c, k)
        return remote(code.at[:, at], rcode.at[:, at], a2_s.at[k], a2_r.at[k], y_id)

    def a2_fwd(core, k):
        at = cols(core, k)
        return remote(rcode.at[:, at], rcode.at[:, at], a2f_s.at[k], a2f_r.at[k], sib_id)

    for k in range(3):
        when_tail(c, k, lambda k=k: a2(k).start())

    loads[1].wait()
    loads[2].wait()
    nt = (((1,), (1,)), ((), ()))
    hi = lax.Precision.HIGHEST
    inner_proj = lax.dot_general(einner[...], bt[...], nt, precision=hi, preferred_element_type=jnp.float32)
    for i in range(groups):
        proj[i] = inner_proj[i * rows_e : (i + 1) * rows_e]
    e_peers = (sib_id, y_id, diag_id)

    def e_copy(i):
        return remote(proj.at[e_peers[i][0]], precv.at[i], e_s.at[i], e_r.at[i], e_peers[i])

    for i in range(3):
        e_copy(i).start()

    loads[3].wait()
    loads[4].wait()

    def update(at, at_io):
        total = decode(code[:, at_io]) + decode(rcode[:, at_io])
        average = w[:, at_io] - total * (1.0 / groups)
        new_v, mom_v = nesterov(w[:, at_io], m[:, at_io], average)
        new[:, at_io] = new_v
        mom[:, at_io] = mom_v
        own[:, at_io] = new_v.astype(jnp.bfloat16)

    def update_cols(core, k):
        if k == 2:
            update(None, pl.ds(tail0, width - tail0))
        else:
            update(None, cols(core, k))

    own[:, tail0:] = jnp.zeros_like(own[:, tail0:])

    def block(zsrc, xsrc, at):
        return all_h.at[zsrc * 2 + xsrc, :, at]

    def z_copy(zsrc, k, sems, peer, src=None):
        at = cols(c, k)
        dst = block(zsrc, x, at)
        return remote(dst if src is None else src.at[:, at], dst, sems.at[zsrc, k], z_r.at[zsrc, k], peer)

    def x_copy(zsrc, k, xsrc, src=None):
        at = cols(c, k)
        dst = block(zsrc, xsrc, at)
        return remote(dst if src is None else src.at[:, at], dst, x_s.at[zsrc, k // 2], x_r.at[zsrc, k // 2], x_id)

    def y_copy(zsrc, k):
        dst = block(zsrc, 1 - x, cols(c, k))
        return remote(dst, dst, y_s.at[zsrc], y_r.at[zsrc], y_id)

    def cz_copy(core, zsrc, k):
        dst = block(zsrc, x, cols(core, k))
        return remote(dst, dst, cz_s.at[zsrc, k], cz_r.at[zsrc, k], sib_id)

    def cx_copy(core, zsrc, k):
        dst = block(zsrc, 1 - x, cols(core, k))
        return remote(dst, dst, cx_s.at[zsrc, k // 2], cx_r.at[zsrc, k // 2], sib_id)

    def cy_copy(core, zsrc):
        dst = block(zsrc, 1 - x, cols(core, 1))
        return remote(dst, dst, cy_s.at[zsrc], cy_r.at[zsrc], sib_id)

    def own_piece(k):
        a2_in(k).wait_recv()
        a2_fwd(c, k).start()
        update_cols(c, k)

        @pl.when(has_up)
        def _():
            z_copy(z, k, up_s, up_id, own).start()

        @pl.when(has_dn)
        def _():
            z_copy(z, k, dn_s, dn_id, own).start()

        if k != 1:
            x_copy(z, k, x, own).start()

    for k in range(3):
        when_tail(c, k, lambda k=k: own_piece(k))

    def other_piece(k):
        a2_fwd(1 - c, k).wait_recv()
        update_cols(1 - c, k)

    for k in range(3):
        when_tail(1 - c, k, lambda k=k: other_piece(k))
    stores = [
        pltpu.make_async_copy(src, dst, out_sem.at[i])
        for i, (src, dst) in enumerate(
            [(own, all_h.at[s]), (new, new_h), (mom, mom_h), (enew, enew_h), (emom, emom_h)]
        )
    ]
    for store in stores[:3]:
        store.start()

    loads[5].wait()
    loads[6].wait()
    own_proj = lax.dot_general(ew[...], bt[...], nt, precision=hi, preferred_element_type=jnp.float32)
    for i in range(3):
        e_copy(i).wait_recv()
    mean_proj = (proj[g] + precv[0] + precv[1] + precv[2]) * (1.0 / groups)
    step = jnp.dot(own_proj - mean_proj, bt[...], precision=hi, preferred_element_type=jnp.float32)
    enew_v, emom_v = nesterov(ew[...], em[...], step)
    enew[...] = enew_v
    emom[...] = emom_v
    for store in stores[3:]:
        store.start()

    def z_arrive(zsrc, k, sems, peer, more):
        z_copy(zsrc, k, sems, peer).wait_recv()

        @pl.when(more)
        def _():
            z_copy(zsrc, k, sems, peer).start()

        if k != 1:
            x_copy(zsrc, k, x).start()
        cz_copy(c, zsrc, k).start()

    def x_arrive(zsrc, k):
        x_copy(zsrc, k, 1 - x).wait_recv()
        if k == 0:
            y_copy(zsrc, 0).start()
        cx_copy(c, zsrc, k).start()

    def y_arrive(zsrc):
        y_copy(zsrc, 1).wait_recv()
        cy_copy(c, zsrc).start()

    def both(d, f):
        @pl.when(z >= d)
        def _():
            f(z - d, up_s, up_id, has_up)

        @pl.when(z + d < zs)
        def _():
            f(z + d, dn_s, dn_id, has_dn)

    def x_all(zsrc):
        x_arrive(zsrc, 0)
        pl.when(c == 1)(lambda: x_arrive(zsrc, 2))

    def steps(d, carry):
        both(d, lambda zsrc, sems, peer, more: z_arrive(zsrc, 0, sems, peer, more))

        @pl.when(d == 1)
        def _():
            x_all(z)

        @pl.when(d == 2)
        def _():
            y_arrive(z)

        @pl.when(d > 1)
        def _():
            both(d - 1, lambda zsrc, sems, peer, more: x_all(zsrc))

        @pl.when(d > 2)
        def _():
            both(d - 2, lambda zsrc, sems, peer, more: y_arrive(zsrc))

        both(d, lambda zsrc, sems, peer, more: z_arrive(zsrc, 1, sems, peer, more))

        @pl.when(c == 1)
        def _():
            both(d, lambda zsrc, sems, peer, more: z_arrive(zsrc, 2, sems, peer, more))

        return carry

    lax.fori_loop(1, zs, steps, 0)
    both(zs - 1, lambda zsrc, sems, peer, more: x_all(zsrc))
    both(zs - 2, lambda zsrc, sems, peer, more: y_arrive(zsrc))
    both(zs - 1, lambda zsrc, sems, peer, more: y_arrive(zsrc))

    def finish(zsrc, carry):
        far = zsrc != z

        def sent(k):
            @pl.when(has_up & (zsrc <= z))
            def _():
                z_copy(zsrc, k, up_s, up_id).wait_send()

            @pl.when(has_dn & (zsrc >= z))
            def _():
                z_copy(zsrc, k, dn_s, dn_id).wait_send()

            if k != 1:
                x_copy(zsrc, k, x).wait_send()
                cx_copy(c, zsrc, k).wait_send()

            @pl.when(far)
            def _():
                cz_copy(c, zsrc, k).wait_send()

        def came(k):
            @pl.when(far)
            def _():
                cz_copy(1 - c, zsrc, k).wait_recv()

            if k != 1:
                cx_copy(1 - c, zsrc, k).wait_recv()

        for k in range(3):
            when_tail(c, k, lambda k=k: sent(k))
            when_tail(1 - c, k, lambda k=k: came(k))
        y_copy(zsrc, 0).wait_send()
        cy_copy(c, zsrc).wait_send()
        cy_copy(1 - c, zsrc).wait_recv()
        return carry

    lax.fori_loop(0, zs, finish, 0)
    a1.wait_send()
    for k in range(3):
        when_tail(c, k, lambda k=k: (a2(k).wait_send(), a2_fwd(c, k).wait_send(), None)[-1])
    for i in range(3):
        e_copy(i).wait_send()
    for store in stores:
        store.wait()


def solution(mesh):
    groups, shards = mesh.shape["grp"], mesh.shape["shard"]
    zs = shards // 2

    def per_device(layer_inner, layer_weights, layer_moment, embed_inner, embed_weights, embed_moment, basis):
        f32, bf16 = jnp.float32, jnp.bfloat16
        rows, width = layer_weights.shape
        rows_g, rows_e = embed_inner.shape[1], embed_weights.shape[0]
        rank = basis.shape[1]
        quarter = width // (4 * LANES) * LANES
        wide = -(-width // LANES) * LANES
        layer, emb = (rows, width), (rows_e, width)
        dma = pltpu.SemaphoreType.DMA
        any_ = pl.BlockSpec(memory_space=pl.ANY)
        new, mom, whole, enew, emom = pl.pallas_call(
            functools.partial(kernel, zs, groups, quarter),
            out_shape=(
                jax.ShapeDtypeStruct(layer, f32),
                jax.ShapeDtypeStruct(layer, f32),
                jax.ShapeDtypeStruct((shards, rows, wide), bf16),
                jax.ShapeDtypeStruct(emb, f32),
                jax.ShapeDtypeStruct(emb, f32),
            ),
            in_specs=[any_] * 7,
            out_specs=(any_,) * 5,
            scratch_shapes=[
                pltpu.VMEM(layer, f32), pltpu.VMEM(layer, f32), pltpu.VMEM(layer, f32), pltpu.VMEM(layer, f32),
                pltpu.VMEM((rows_g, width), f32), pltpu.VMEM(emb, f32), pltpu.VMEM(emb, f32),
                pltpu.VMEM((rank, width), f32),
                pltpu.VMEM((rows, wide), bf16), pltpu.VMEM((rows, wide), bf16), pltpu.VMEM((rows, wide), bf16),
                pltpu.VMEM(layer, f32), pltpu.VMEM(layer, f32),
                pltpu.VMEM((groups, rows_e, rank), f32), pltpu.VMEM((3, rows_e, rank), f32),
                pltpu.VMEM(emb, f32), pltpu.VMEM(emb, f32),
                dma((7,)), dma((5,)), dma, dma, dma((3,)), dma((3,)), dma((3,)), dma((3,)), dma((3,)), dma((3,)),
                dma((zs, 3)), dma((zs, 3)), dma((zs, 3)), dma((zs, 2)), dma((zs, 2)), dma((zs,)), dma((zs,)),
                dma((zs, 3)), dma((zs, 3)), dma((zs, 2)), dma((zs, 2)), dma((zs,)), dma((zs,)),
            ],
            compiler_params=pltpu.CompilerParams(
                collective_id=0, has_side_effects=True, vmem_limit_bytes=40 * 1024 * 1024
            ),
        )(layer_inner, layer_weights, layer_moment, embed_inner, embed_weights, embed_moment, basis.T)
        layer_copy = whole[:, :, :width].reshape(shards * rows, width)
        return new, mom, layer_copy, enew, emom

    in_specs = (
        P("grp", "shard", None),
        P("shard", None),
        P("shard", None),
        P("grp", "shard", None),
        P(("shard", "grp"), None),
        P(("shard", "grp"), None),
        P(),
    )
    out_specs = (
        P("shard", None),
        P("shard", None),
        P(),
        P(("shard", "grp"), None),
        P(("shard", "grp"), None),
    )
    return jax.shard_map(
        per_device, mesh=mesh, in_specs=in_specs, out_specs=out_specs, check_vma=False
    )
```

```python
import functools

import jax
import jax.numpy as jnp
from jax import lax
from jax.experimental import pallas as pl
from jax.experimental.pallas import tpu as pltpu
from jax.sharding import PartitionSpec as P

outer_rate = 0.7
momentum_coef = 0.9
MESH = pl.DeviceIdType.MESH
LANES = 128
VMEM_LIMIT = 24 * 1024 * 1024
SLOPE = 13.0
SHIFT = 78.0


def nesterov(weights, moment, average):
    moment_new = momentum_coef * moment + average
    return (weights - outer_rate * (average + momentum_coef * moment_new), moment_new)


def encode(x):
    size = jnp.exp(jnp.abs(x) * SLOPE - SHIFT)
    return jnp.where(x < 0, -size, size).astype(jnp.bfloat16)


def decode(code):
    code = code.astype(jnp.float32)
    size = (jnp.log(jnp.abs(code)) + SHIFT) * (1.0 / SLOPE)
    return jnp.where(code < 0, -size, size)


def split(a):
    high = a.astype(jnp.bfloat16)
    return high, (a - high.astype(jnp.float32)).astype(jnp.bfloat16)


def kernel(
    zs, groups, quarter,
    inner_h, w_h, m_h, einner_h, ew_h, em_h, bt_h,
    new_h, mom_h, all_h, enew_h, emom_h,
    inner, sib, w, m, einner, ew, em, bt, code, rcode, own, new, mom, proj, precv, enew, emom,
    in_sem, out_sem, a1_s, a1_r, a2_s, a2_r, a2f_s, a2f_r, e_s, e_r,
    up_s, dn_s, z_r, x_s, x_r, y_s, y_r, cz_s, cz_r, cx_s, cx_r, cy_s, cy_r,
):
    g, s = lax.axis_index("grp"), lax.axis_index("shard")
    y, c = g // 2, g % 2
    z, x = s // 2, s % 2
    width = inner_h.shape[-1]
    rows_e = ew_h.shape[0]
    tail0 = 4 * quarter
    tail_w = own.shape[-1] - tail0
    sib_id = (y * 2 + 1 - c, s)
    y_id = ((1 - y) * 2 + c, s)
    diag_id = ((1 - y) * 2 + 1 - c, s)
    x_id = (g, z * 2 + 1 - x)
    up_id = (g, s + 2)
    dn_id = (g, s - 2)
    has_up, has_dn = z < zs - 1, z > 0

    loads = [
        pltpu.make_async_copy(src, dst, in_sem.at[i])
        for i, (src, dst) in enumerate(
            [(inner_h.at[0], inner), (einner_h.at[0], einner), (bt_h, bt), (w_h, w), (m_h, m), (ew_h, ew), (em_h, em)]
        )
    ]
    for load in loads:
        load.start()

    barrier = pltpu.get_barrier_semaphore()
    for peer in (sib_id, y_id, diag_id, x_id):
        pl.semaphore_signal(barrier, inc=1, device_id=peer, device_id_type=MESH)

    @pl.when(has_up)
    def _():
        pl.semaphore_signal(barrier, inc=1, device_id=up_id, device_id_type=MESH)

    @pl.when(has_dn)
    def _():
        pl.semaphore_signal(barrier, inc=1, device_id=dn_id, device_id_type=MESH)

    pl.semaphore_wait(barrier, 4 + has_up.astype(jnp.int32) + has_dn.astype(jnp.int32))

    def remote(src, dst, ssem, rsem, peer):
        return pltpu.make_async_remote_copy(
            src_ref=src, dst_ref=dst, send_sem=ssem, recv_sem=rsem, device_id=peer, device_id_type=MESH
        )

    def a1(i, receiver):
        if i == 1:
            at = pl.ds(tail0, width - tail0)
        else:
            core = receiver if i == 0 else 1 - receiver
            at = pl.ds(pl.multiple_of(core * 2 * quarter, LANES), 2 * quarter)
        return remote(inner_h.at[0, :, at], sib.at[:, at], a1_s.at[i], a1_r.at[i], sib_id)

    for i in range(3):
        a1(i, 1 - c).start()
    code[:, tail0:] = jnp.zeros_like(code[:, tail0:])

    def cols(core, k):
        if k == 2:
            return pl.ds(tail0, tail_w)
        return pl.ds(pl.multiple_of((core * 2 + (y if k == 0 else 1 - y)) * quarter, LANES), quarter)

    def when_tail(core, k, f):
        if k == 2:
            pl.when(core == 1)(f)
        else:
            f()

    def a2(k):
        at = cols(c, 1 - k if k < 2 else 2)
        return remote(code.at[:, at], rcode.at[:, at], a2_s.at[k], a2_r.at[k], y_id)

    def a2_in(k):
        at = cols(c, k)
        return remote(code.at[:, at], rcode.at[:, at], a2_s.at[k], a2_r.at[k], y_id)

    def a2_fwd(core, k):
        at = cols(core, k)
        return remote(rcode.at[:, at], rcode.at[:, at], a2f_s.at[k], a2f_r.at[k], sib_id)

    def add_pair(at):
        code[:, at] = encode(inner[:, at] + sib[:, at])

    loads[0].wait()
    a1(0, c).wait_recv()
    for k in range(2):
        add_pair(cols(c, 1 - k))
        a2(k).start()
    a1(1, c).wait_recv()
    add_pair(pl.ds(tail0, width - tail0))
    pl.when(c == 1)(lambda: a2(2).start())

    loads[1].wait()
    loads[2].wait()
    nt = (((1,), (1,)), ((), ()))
    basis_parts = jnp.concatenate(split(bt[...]), axis=0)
    rank = bt.shape[0]

    def project(a):
        total = 0.0
        for part in split(a):
            both_parts = lax.dot_general(part, basis_parts, nt, preferred_element_type=jnp.float32)
            total = total + (both_parts[:, :rank] + both_parts[:, rank:])
        return total

    inner_proj = project(einner[...])
    for i in range(groups):
        proj[i] = inner_proj[i * rows_e : (i + 1) * rows_e]
    e_peers = (sib_id, y_id, diag_id)

    def e_copy(i):
        return remote(proj.at[e_peers[i][0]], precv.at[i], e_s.at[i], e_r.at[i], e_peers[i])

    for i in range(3):
        e_copy(i).start()
    a1(2, c).wait_recv()
    add_pair(pl.ds(pl.multiple_of((1 - c) * 2 * quarter, LANES), 2 * quarter))

    loads[3].wait()
    loads[4].wait()

    def update(at, at_io):
        total = decode(code[:, at_io]) + decode(rcode[:, at_io])
        average = w[:, at_io] - total * (1.0 / groups)
        new_v, mom_v = nesterov(w[:, at_io], m[:, at_io], average)
        new[:, at_io] = new_v
        mom[:, at_io] = mom_v
        own[:, at_io] = new_v.astype(jnp.bfloat16)

    def update_cols(core, k):
        if k == 2:
            update(None, pl.ds(tail0, width - tail0))
        else:
            update(None, cols(core, k))

    own[:, tail0:] = jnp.zeros_like(own[:, tail0:])

    def block(zsrc, xsrc, at):
        return all_h.at[zsrc * 2 + xsrc, :, at]

    def z_copy(zsrc, k, sems, peer, src=None):
        at = cols(c, k)
        dst = block(zsrc, x, at)
        return remote(dst if src is None else src.at[:, at], dst, sems.at[zsrc, k], z_r.at[zsrc, k], peer)

    def x_copy(zsrc, k, xsrc, src=None):
        at = cols(c, k)
        dst = block(zsrc, xsrc, at)
        return remote(dst if src is None else src.at[:, at], dst, x_s.at[zsrc, k // 2], x_r.at[zsrc, k // 2], x_id)

    def y_copy(zsrc, k):
        dst = block(zsrc, 1 - x, cols(c, k))
        return remote(dst, dst, y_s.at[zsrc], y_r.at[zsrc], y_id)

    def cz_copy(core, zsrc, k):
        dst = block(zsrc, x, cols(core, k))
        return remote(dst, dst, cz_s.at[zsrc, k], cz_r.at[zsrc, k], sib_id)

    def cx_copy(core, zsrc, k):
        dst = block(zsrc, 1 - x, cols(core, k))
        return remote(dst, dst, cx_s.at[zsrc, k // 2], cx_r.at[zsrc, k // 2], sib_id)

    def cy_copy(core, zsrc):
        dst = block(zsrc, 1 - x, cols(core, 1))
        return remote(dst, dst, cy_s.at[zsrc], cy_r.at[zsrc], sib_id)

    def own_piece(k):
        a2_in(k).wait_recv()
        a2_fwd(c, k).start()
        update_cols(c, k)

        @pl.when(has_up)
        def _():
            z_copy(z, k, up_s, up_id, own).start()

        @pl.when(has_dn)
        def _():
            z_copy(z, k, dn_s, dn_id, own).start()

        if k != 1:
            x_copy(z, k, x, own).start()

    for k in range(3):
        when_tail(c, k, lambda k=k: own_piece(k))

    def other_piece(k):
        a2_fwd(1 - c, k).wait_recv()
        update_cols(1 - c, k)

    for k in range(3):
        when_tail(1 - c, k, lambda k=k: other_piece(k))
    stores = [
        pltpu.make_async_copy(src, dst, out_sem.at[i])
        for i, (src, dst) in enumerate(
            [(own, all_h.at[s]), (new, new_h), (mom, mom_h), (enew, enew_h), (emom, emom_h)]
        )
    ]
    for store in stores[:3]:
        store.start()

    loads[5].wait()
    loads[6].wait()
    own_proj = project(ew[...])
    for i in range(3):
        e_copy(i).wait_recv()
    mean_proj = (proj[g] + precv[0] + precv[1] + precv[2]) * (1.0 / groups)
    high, low = split(own_proj - mean_proj)
    step = jnp.dot(
        jnp.concatenate([high, high, low, low], axis=1),
        jnp.concatenate([basis_parts, basis_parts], axis=0),
        preferred_element_type=jnp.float32,
    )
    enew_v, emom_v = nesterov(ew[...], em[...], step)
    enew[...] = enew_v
    emom[...] = emom_v
    for store in stores[3:]:
        store.start()

    def z_arrive(zsrc, k, sems, peer, more):
        z_copy(zsrc, k, sems, peer).wait_recv()

        @pl.when(more)
        def _():
            z_copy(zsrc, k, sems, peer).start()

        if k != 1:
            x_copy(zsrc, k, x).start()
        cz_copy(c, zsrc, k).start()

    def x_arrive(zsrc, k):
        x_copy(zsrc, k, 1 - x).wait_recv()
        if k == 0:
            y_copy(zsrc, 0).start()
        cx_copy(c, zsrc, k).start()

    def y_arrive(zsrc):
        y_copy(zsrc, 1).wait_recv()
        cy_copy(c, zsrc).start()

    def both(d, f):
        @pl.when(z >= d)
        def _():
            f(z - d, up_s, up_id, has_up)

        @pl.when(z + d < zs)
        def _():
            f(z + d, dn_s, dn_id, has_dn)

    def x_all(zsrc):
        x_arrive(zsrc, 0)
        pl.when(c == 1)(lambda: x_arrive(zsrc, 2))

    def steps(d, carry):
        both(d, lambda zsrc, sems, peer, more: z_arrive(zsrc, 0, sems, peer, more))

        @pl.when(d == 1)
        def _():
            x_all(z)

        @pl.when(d == 2)
        def _():
            y_arrive(z)

        @pl.when(d > 1)
        def _():
            both(d - 1, lambda zsrc, sems, peer, more: x_all(zsrc))

        @pl.when(d > 2)
        def _():
            both(d - 2, lambda zsrc, sems, peer, more: y_arrive(zsrc))

        both(d, lambda zsrc, sems, peer, more: z_arrive(zsrc, 1, sems, peer, more))

        @pl.when(c == 1)
        def _():
            both(d, lambda zsrc, sems, peer, more: z_arrive(zsrc, 2, sems, peer, more))

        return carry

    lax.fori_loop(1, zs, steps, 0)
    both(zs - 1, lambda zsrc, sems, peer, more: x_all(zsrc))
    both(zs - 2, lambda zsrc, sems, peer, more: y_arrive(zsrc))
    both(zs - 1, lambda zsrc, sems, peer, more: y_arrive(zsrc))

    def finish(zsrc, carry):
        far = zsrc != z

        def sent(k):
            @pl.when(has_up & (zsrc <= z))
            def _():
                z_copy(zsrc, k, up_s, up_id).wait_send()

            @pl.when(has_dn & (zsrc >= z))
            def _():
                z_copy(zsrc, k, dn_s, dn_id).wait_send()

            if k != 1:
                x_copy(zsrc, k, x).wait_send()
                cx_copy(c, zsrc, k).wait_send()

            @pl.when(far)
            def _():
                cz_copy(c, zsrc, k).wait_send()

        def came(k):
            @pl.when(far)
            def _():
                cz_copy(1 - c, zsrc, k).wait_recv()

            if k != 1:
                cx_copy(1 - c, zsrc, k).wait_recv()

        for k in range(3):
            when_tail(c, k, lambda k=k: sent(k))
            when_tail(1 - c, k, lambda k=k: came(k))
        y_copy(zsrc, 0).wait_send()
        cy_copy(c, zsrc).wait_send()
        cy_copy(1 - c, zsrc).wait_recv()
        return carry

    lax.fori_loop(0, zs, finish, 0)
    for i in range(3):
        a1(i, 1 - c).wait_send()
    for k in range(3):
        when_tail(c, k, lambda k=k: (a2(k).wait_send(), a2_fwd(c, k).wait_send(), None)[-1])
    for i in range(3):
        e_copy(i).wait_send()
    for store in stores:
        store.wait()


def solution(mesh):
    groups, shards = mesh.shape["grp"], mesh.shape["shard"]
    zs = shards // 2

    def per_device(layer_inner, layer_weights, layer_moment, embed_inner, embed_weights, embed_moment, basis):
        f32, bf16 = jnp.float32, jnp.bfloat16
        rows, width = layer_weights.shape
        rows_g, rows_e = embed_inner.shape[1], embed_weights.shape[0]
        rank = basis.shape[1]
        quarter = width // (4 * LANES) * LANES
        wide = -(-width // LANES) * LANES
        layer, emb = (rows, width), (rows_e, width)
        dma = pltpu.SemaphoreType.DMA
        operands = [
            pltpu.with_memory_space_constraint(a, pltpu.HBM)
            for a in (layer_inner, layer_weights, layer_moment, embed_inner, embed_weights, embed_moment, basis.T)
        ]
        any_ = pl.BlockSpec(memory_space=pl.ANY)
        new, mom, whole, enew, emom = pl.pallas_call(
            functools.partial(kernel, zs, groups, quarter),
            out_shape=(
                jax.ShapeDtypeStruct(layer, f32),
                jax.ShapeDtypeStruct(layer, f32),
                jax.ShapeDtypeStruct((shards, rows, wide), bf16),
                jax.ShapeDtypeStruct(emb, f32),
                jax.ShapeDtypeStruct(emb, f32),
            ),
            in_specs=[pl.BlockSpec(memory_space=pltpu.HBM)] * 7,
            out_specs=(any_,) * 5,
            scratch_shapes=[
                pltpu.VMEM(layer, f32), pltpu.VMEM(layer, f32), pltpu.VMEM(layer, f32), pltpu.VMEM(layer, f32),
                pltpu.VMEM((rows_g, width), f32), pltpu.VMEM(emb, f32), pltpu.VMEM(emb, f32),
                pltpu.VMEM((rank, width), f32),
                pltpu.VMEM((rows, wide), bf16), pltpu.VMEM((rows, wide), bf16), pltpu.VMEM((rows, wide), bf16),
                pltpu.VMEM(layer, f32), pltpu.VMEM(layer, f32),
                pltpu.VMEM((groups, rows_e, rank), f32), pltpu.VMEM((3, rows_e, rank), f32),
                pltpu.VMEM(emb, f32), pltpu.VMEM(emb, f32),
                dma((7,)), dma((5,)), dma((3,)), dma((3,)), dma((3,)), dma((3,)), dma((3,)), dma((3,)), dma((3,)), dma((3,)),
                dma((zs, 3)), dma((zs, 3)), dma((zs, 3)), dma((zs, 2)), dma((zs, 2)), dma((zs,)), dma((zs,)),
                dma((zs, 3)), dma((zs, 3)), dma((zs, 2)), dma((zs, 2)), dma((zs,)), dma((zs,)),
            ],
            compiler_params=pltpu.CompilerParams(
                collective_id=0, has_side_effects=True, vmem_limit_bytes=VMEM_LIMIT
            ),
        )(*operands)
        layer_copy = whole[:, :, :width].reshape(shards * rows, width)
        return new, mom, layer_copy, enew, emom

    in_specs = (
        P("grp", "shard", None),
        P("shard", None),
        P("shard", None),
        P("grp", "shard", None),
        P(("shard", "grp"), None),
        P(("shard", "grp"), None),
        P(),
    )
    out_specs = (
        P("shard", None),
        P("shard", None),
        P(),
        P(("shard", "grp"), None),
        P(("shard", "grp"), None),
    )
    return jax.shard_map(
        per_device, mesh=mesh, in_specs=in_specs, out_specs=out_specs, check_vma=False
    )
```

```python
import functools

import jax
import jax.numpy as jnp
from jax import lax
from jax.experimental import pallas as pl
from jax.experimental.pallas import tpu as pltpu
from jax.sharding import PartitionSpec as P

outer_rate = 0.7
momentum_coef = 0.9
MESH = pl.DeviceIdType.MESH
LANES = 128
VMEM_LIMIT = 24 * 1024 * 1024
SLOPE = 13.0
SHIFT = 78.0


def nesterov(weights, moment, average):
    moment_new = momentum_coef * moment + average
    return (weights - outer_rate * (average + momentum_coef * moment_new), moment_new)


def encode(x):
    size = jnp.exp(jnp.abs(x) * SLOPE - SHIFT)
    return jnp.where(x < 0, -size, size).astype(jnp.bfloat16)


def decode(code):
    code = code.astype(jnp.float32)
    size = (jnp.log(jnp.abs(code)) + SHIFT) * (1.0 / SLOPE)
    return jnp.where(code < 0, -size, size)


def split(a):
    high = a.astype(jnp.bfloat16)
    return high, (a - high.astype(jnp.float32)).astype(jnp.bfloat16)


def kernel(
    zs, groups, quarter,
    inner_h, w_h, m_h, einner_h, ew_h, em_h, bt_h,
    new_h, mom_h, all_h, enew_h, emom_h,
    inner, sib, w, m, einner, ew, em, bt, code, rcode, own, new, mom, proj, precv, enew, emom,
    in_sem, out_sem, a1_s, a1_r, a2_s, a2_r, a2f_s, a2f_r, e_s, e_r,
    up_s, dn_s, z_r, x_s, x_r, y_s, y_r, cz_s, cz_r, cx_s, cx_r, cy_s, cy_r,
):
    g, s = lax.axis_index("grp"), lax.axis_index("shard")
    y, c = g // 2, g % 2
    z, x = s // 2, s % 2
    width = inner_h.shape[-1]
    rows_e = ew_h.shape[0]
    tail0 = 4 * quarter
    tail_w = own.shape[-1] - tail0
    sib_id = (y * 2 + 1 - c, s)
    y_id = ((1 - y) * 2 + c, s)
    diag_id = ((1 - y) * 2 + 1 - c, s)
    x_id = (g, z * 2 + 1 - x)
    up_id = (g, s + 2)
    dn_id = (g, s - 2)
    has_up, has_dn = z < zs - 1, z > 0

    loads = [
        pltpu.make_async_copy(src, dst, in_sem.at[i])
        for i, (src, dst) in enumerate(
            [(inner_h.at[0], inner), (einner_h.at[0], einner), (bt_h, bt), (w_h, w), (m_h, m), (ew_h, ew), (em_h, em)]
        )
    ]
    for load in loads:
        load.start()

    barrier = pltpu.get_barrier_semaphore()
    for peer in (sib_id, y_id, diag_id, x_id):
        pl.semaphore_signal(barrier, inc=1, device_id=peer, device_id_type=MESH)

    @pl.when(has_up)
    def _():
        pl.semaphore_signal(barrier, inc=1, device_id=up_id, device_id_type=MESH)

    @pl.when(has_dn)
    def _():
        pl.semaphore_signal(barrier, inc=1, device_id=dn_id, device_id_type=MESH)

    pl.semaphore_wait(barrier, 4 + has_up.astype(jnp.int32) + has_dn.astype(jnp.int32))

    def remote(src, dst, ssem, rsem, peer):
        return pltpu.make_async_remote_copy(
            src_ref=src, dst_ref=dst, send_sem=ssem, recv_sem=rsem, device_id=peer, device_id_type=MESH
        )

    def a1(i, receiver):
        if i == 1:
            at = pl.ds(tail0, width - tail0)
        else:
            core = receiver if i == 0 else 1 - receiver
            at = pl.ds(pl.multiple_of(core * 2 * quarter, LANES), 2 * quarter)
        return remote(inner_h.at[0, :, at], sib.at[:, at], a1_s.at[i], a1_r.at[i], sib_id)

    for i in range(3):
        a1(i, 1 - c).start()
    code[:, tail0:] = jnp.zeros_like(code[:, tail0:])

    def cols(core, k):
        if k == 2:
            return pl.ds(tail0, tail_w)
        return pl.ds(pl.multiple_of((core * 2 + (y if k == 0 else 1 - y)) * quarter, LANES), quarter)

    def when_tail(core, k, f):
        if k == 2:
            pl.when(core == 1)(f)
        else:
            f()

    def a2(k):
        at = cols(c, 1 - k if k < 2 else 2)
        return remote(code.at[:, at], rcode.at[:, at], a2_s.at[k], a2_r.at[k], y_id)

    def a2_in(k):
        at = cols(c, k)
        return remote(code.at[:, at], rcode.at[:, at], a2_s.at[k], a2_r.at[k], y_id)

    def a2_fwd(core, k):
        at = cols(core, k)
        return remote(rcode.at[:, at], rcode.at[:, at], a2f_s.at[k], a2f_r.at[k], sib_id)

    def add_pair(at):
        code[:, at] = encode(inner[:, at] + sib[:, at])

    loads[0].wait()
    a1(0, c).wait_recv()
    for k in range(2):
        add_pair(cols(c, 1 - k))
        a2(k).start()
    a1(1, c).wait_recv()
    add_pair(pl.ds(tail0, width - tail0))
    pl.when(c == 1)(lambda: a2(2).start())

    loads[1].wait()
    loads[2].wait()
    nt = (((1,), (1,)), ((), ()))
    basis_parts = jnp.concatenate(split(bt[...]), axis=0)
    rank = bt.shape[0]

    def project(a):
        total = 0.0
        for part in split(a):
            both_parts = lax.dot_general(part, basis_parts, nt, preferred_element_type=jnp.float32)
            total = total + (both_parts[:, :rank] + both_parts[:, rank:])
        return total

    inner_proj = project(einner[...])
    for i in range(groups):
        proj[i] = inner_proj[i * rows_e : (i + 1) * rows_e]
    e_peers = (sib_id, y_id, diag_id)

    def e_copy(i):
        return remote(proj.at[e_peers[i][0]], precv.at[i], e_s.at[i], e_r.at[i], e_peers[i])

    for i in range(3):
        e_copy(i).start()
    a1(2, c).wait_recv()
    add_pair(pl.ds(pl.multiple_of((1 - c) * 2 * quarter, LANES), 2 * quarter))

    loads[3].wait()
    loads[4].wait()

    def update(at, at_io):
        total = decode(code[:, at_io]) + decode(rcode[:, at_io])
        average = w[:, at_io] - total * (1.0 / groups)
        new_v, mom_v = nesterov(w[:, at_io], m[:, at_io], average)
        new[:, at_io] = new_v
        mom[:, at_io] = mom_v
        own[:, at_io] = new_v.astype(jnp.bfloat16)

    def update_cols(core, k):
        if k == 2:
            update(None, pl.ds(tail0, width - tail0))
        else:
            update(None, cols(core, k))

    own[:, tail0:] = jnp.zeros_like(own[:, tail0:])

    def block(zsrc, xsrc, at):
        return all_h.at[zsrc * 2 + xsrc, :, at]

    def z_copy(zsrc, k, sems, peer, src=None):
        at = cols(c, k)
        dst = block(zsrc, x, at)
        return remote(dst if src is None else src.at[:, at], dst, sems.at[zsrc, k], z_r.at[zsrc, k], peer)

    def x_copy(zsrc, k, xsrc, src=None):
        at = cols(c, k)
        dst = block(zsrc, xsrc, at)
        return remote(dst if src is None else src.at[:, at], dst, x_s.at[zsrc, k // 2], x_r.at[zsrc, k // 2], x_id)

    def y_copy(zsrc, k):
        dst = block(zsrc, 1 - x, cols(c, k))
        return remote(dst, dst, y_s.at[zsrc], y_r.at[zsrc], y_id)

    def cz_copy(core, zsrc, k):
        dst = block(zsrc, x, cols(core, k))
        return remote(dst, dst, cz_s.at[zsrc, k], cz_r.at[zsrc, k], sib_id)

    def cx_copy(core, zsrc, k):
        dst = block(zsrc, 1 - x, cols(core, k))
        return remote(dst, dst, cx_s.at[zsrc, k // 2], cx_r.at[zsrc, k // 2], sib_id)

    def cy_copy(core, zsrc):
        dst = block(zsrc, 1 - x, cols(core, 1))
        return remote(dst, dst, cy_s.at[zsrc], cy_r.at[zsrc], sib_id)

    def own_piece(k):
        a2_in(k).wait_recv()
        a2_fwd(c, k).start()
        update_cols(c, k)

        @pl.when(has_up)
        def _():
            z_copy(z, k, up_s, up_id, own).start()

        @pl.when(has_dn)
        def _():
            z_copy(z, k, dn_s, dn_id, own).start()

        if k != 1:
            x_copy(z, k, x, own).start()

    for k in range(3):
        when_tail(c, k, lambda k=k: own_piece(k))

    def other_piece(k):
        a2_fwd(1 - c, k).wait_recv()
        update_cols(1 - c, k)

    for k in range(3):
        when_tail(1 - c, k, lambda k=k: other_piece(k))
    stores = [
        pltpu.make_async_copy(src, dst, out_sem.at[i])
        for i, (src, dst) in enumerate(
            [(own, all_h.at[s]), (new, new_h), (mom, mom_h), (enew, enew_h), (emom, emom_h)]
        )
    ]
    for store in stores[:3]:
        store.start()

    loads[5].wait()
    loads[6].wait()
    own_proj = project(ew[...])
    for i in range(3):
        e_copy(i).wait_recv()
    mean_proj = (proj[g] + precv[0] + precv[1] + precv[2]) * (1.0 / groups)
    high, low = split(own_proj - mean_proj)
    step = jnp.dot(
        jnp.concatenate([high, high, low, low], axis=1),
        jnp.concatenate([basis_parts, basis_parts], axis=0),
        preferred_element_type=jnp.float32,
    )
    enew_v, emom_v = nesterov(ew[...], em[...], step)
    enew[...] = enew_v
    emom[...] = emom_v
    for store in stores[3:]:
        store.start()

    def z_arrive(zsrc, k, sems, peer, more):
        z_copy(zsrc, k, sems, peer).wait_recv()

        @pl.when(more)
        def _():
            z_copy(zsrc, k, sems, peer).start()

        if k != 1:
            x_copy(zsrc, k, x).start()
        cz_copy(c, zsrc, k).start()

    def x_arrive(zsrc, k):
        x_copy(zsrc, k, 1 - x).wait_recv()
        if k == 0:
            y_copy(zsrc, 0).start()
        cx_copy(c, zsrc, k).start()

    def y_arrive(zsrc):
        y_copy(zsrc, 1).wait_recv()
        cy_copy(c, zsrc).start()

    def both(d, f):
        @pl.when(z >= d)
        def _():
            f(z - d, up_s, up_id, has_up)

        @pl.when(z + d < zs)
        def _():
            f(z + d, dn_s, dn_id, has_dn)

    def x_all(zsrc):
        x_arrive(zsrc, 0)
        pl.when(c == 1)(lambda: x_arrive(zsrc, 2))

    def steps(d, carry):
        both(d, lambda zsrc, sems, peer, more: z_arrive(zsrc, 0, sems, peer, more))

        @pl.when(d == 1)
        def _():
            x_all(z)

        @pl.when(d == 2)
        def _():
            y_arrive(z)

        @pl.when(d > 1)
        def _():
            both(d - 1, lambda zsrc, sems, peer, more: x_all(zsrc))

        @pl.when(d > 2)
        def _():
            both(d - 2, lambda zsrc, sems, peer, more: y_arrive(zsrc))

        both(d, lambda zsrc, sems, peer, more: z_arrive(zsrc, 1, sems, peer, more))

        @pl.when(c == 1)
        def _():
            both(d, lambda zsrc, sems, peer, more: z_arrive(zsrc, 2, sems, peer, more))

        return carry

    lax.fori_loop(1, zs, steps, 0)
    both(zs - 1, lambda zsrc, sems, peer, more: x_all(zsrc))
    both(zs - 2, lambda zsrc, sems, peer, more: y_arrive(zsrc))
    both(zs - 1, lambda zsrc, sems, peer, more: y_arrive(zsrc))

    def finish(zsrc, carry):
        far = zsrc != z

        def sent(k):
            @pl.when(has_up & (zsrc <= z))
            def _():
                z_copy(zsrc, k, up_s, up_id).wait_send()

            @pl.when(has_dn & (zsrc >= z))
            def _():
                z_copy(zsrc, k, dn_s, dn_id).wait_send()

            if k != 1:
                x_copy(zsrc, k, x).wait_send()
                cx_copy(c, zsrc, k).wait_send()

            @pl.when(far)
            def _():
                cz_copy(c, zsrc, k).wait_send()

        def came(k):
            @pl.when(far)
            def _():
                cz_copy(1 - c, zsrc, k).wait_recv()

            if k != 1:
                cx_copy(1 - c, zsrc, k).wait_recv()

        for k in range(3):
            when_tail(c, k, lambda k=k: sent(k))
            when_tail(1 - c, k, lambda k=k: came(k))
        y_copy(zsrc, 0).wait_send()
        cy_copy(c, zsrc).wait_send()
        cy_copy(1 - c, zsrc).wait_recv()
        return carry

    lax.fori_loop(0, zs, finish, 0)
    for i in range(3):
        a1(i, 1 - c).wait_send()
    for k in range(3):
        when_tail(c, k, lambda k=k: (a2(k).wait_send(), a2_fwd(c, k).wait_send(), None)[-1])
    for i in range(3):
        e_copy(i).wait_send()
    for store in stores:
        store.wait()


def store_all(*refs):
    sems = refs[-1]
    count = len(refs) // 2
    copies = [pltpu.make_async_copy(refs[i], refs[count + i], sems.at[i]) for i in range(count)]
    for copy in copies:
        copy.start()
    for copy in copies:
        copy.wait()


def solution(mesh):
    groups, shards = mesh.shape["grp"], mesh.shape["shard"]
    zs = shards // 2

    def per_device(layer_inner, layer_weights, layer_moment, embed_inner, embed_weights, embed_moment, basis):
        f32, bf16 = jnp.float32, jnp.bfloat16
        rows, width = layer_weights.shape
        rows_g, rows_e = embed_inner.shape[1], embed_weights.shape[0]
        rank = basis.shape[1]
        quarter = width // (4 * LANES) * LANES
        wide = -(-width // LANES) * LANES
        layer, emb = (rows, width), (rows_e, width)
        dma = pltpu.SemaphoreType.DMA
        operands = [
            pltpu.with_memory_space_constraint(a, pltpu.HBM)
            for a in (layer_inner, layer_weights, layer_moment, embed_inner, embed_weights, embed_moment, basis.T)
        ]
        any_ = pl.BlockSpec(memory_space=pl.ANY)
        new, mom, whole, enew, emom = pl.pallas_call(
            functools.partial(kernel, zs, groups, quarter),
            out_shape=(
                jax.ShapeDtypeStruct(layer, f32),
                jax.ShapeDtypeStruct(layer, f32),
                jax.ShapeDtypeStruct((shards, rows, wide), bf16),
                jax.ShapeDtypeStruct(emb, f32),
                jax.ShapeDtypeStruct(emb, f32),
            ),
            in_specs=[pl.BlockSpec(memory_space=pltpu.HBM)] * 7,
            out_specs=(any_,) * 5,
            scratch_shapes=[
                pltpu.VMEM(layer, f32), pltpu.VMEM(layer, f32), pltpu.VMEM(layer, f32), pltpu.VMEM(layer, f32),
                pltpu.VMEM((rows_g, width), f32), pltpu.VMEM(emb, f32), pltpu.VMEM(emb, f32),
                pltpu.VMEM((rank, width), f32),
                pltpu.VMEM((rows, wide), bf16), pltpu.VMEM((rows, wide), bf16), pltpu.VMEM((rows, wide), bf16),
                pltpu.VMEM(layer, f32), pltpu.VMEM(layer, f32),
                pltpu.VMEM((groups, rows_e, rank), f32), pltpu.VMEM((3, rows_e, rank), f32),
                pltpu.VMEM(emb, f32), pltpu.VMEM(emb, f32),
                dma((7,)), dma((5,)), dma((3,)), dma((3,)), dma((3,)), dma((3,)), dma((3,)), dma((3,)), dma((3,)), dma((3,)),
                dma((zs, 3)), dma((zs, 3)), dma((zs, 3)), dma((zs, 2)), dma((zs, 2)), dma((zs,)), dma((zs,)),
                dma((zs, 3)), dma((zs, 3)), dma((zs, 2)), dma((zs, 2)), dma((zs,)), dma((zs,)),
            ],
            compiler_params=pltpu.CompilerParams(
                collective_id=0, has_side_effects=True, vmem_limit_bytes=VMEM_LIMIT
            ),
        )(*operands)
        new, mom, enew, emom = pl.pallas_call(
            store_all,
            out_shape=[jax.ShapeDtypeStruct(shape, f32) for shape in (layer, layer, emb, emb)],
            in_specs=[any_] * 4,
            out_specs=[any_] * 4,
            scratch_shapes=[dma((4,))],
            compiler_params=pltpu.CompilerParams(vmem_limit_bytes=1024 * 1024),
        )(new, mom, enew, emom)
        layer_copy = whole[:, :, :width].reshape(shards * rows, width)
        return new, mom, layer_copy, enew, emom

    in_specs = (
        P("grp", "shard", None),
        P("shard", None),
        P("shard", None),
        P("grp", "shard", None),
        P(("shard", "grp"), None),
        P(("shard", "grp"), None),
        P(),
    )
    out_specs = (
        P("shard", None),
        P("shard", None),
        P(),
        P(("shard", "grp"), None),
        P(("shard", "grp"), None),
    )
    return jax.shard_map(
        per_device, mesh=mesh, in_specs=in_specs, out_specs=out_specs, check_vma=False
    )
```
